1024 devices in a mesh: dp: 64 (over z_lo, x, core), mp: 16 (over z_hi, y).
Axes of the slice: x: 4, y: 4, z: 32 (z_hi: 4, z_lo: 8; z = z_hi * 8 + z_lo), core: 2. Of those that a mesh axis runs over, the one named last changes fastest.
Arguments:
- inputs: bfloat16 [2048, 6144], P('dp', 'mp'), may hold values from -6 to 6
- act_grad: bfloat16 [2048, 24576], P('mp', 'dp'), may hold values from -6 to 6
- w_in: bfloat16 [6144, 24576], P('mp', 'dp'), may hold values from -0.078125 to 0.078125
- bias_in: float32 [24576], P('dp'), may hold values from -5 to 5
Outputs:
- input_grad: bfloat16 [2048, 6144], P('dp', 'mp')
- w_in_grad: float32 [6144, 24576], P('mp', 'dp')
- bias_grad: float32 [24576], P('dp')
The draws below stay inside these ranges and needn't reach their ends.
All inputs are finite; a program needn't handle non-finite values.
Results may differ from the reference program's by a relative error of at most 0.017.
Values may be sent and summed in bfloat16 or wider, within the bound.
A program may use at most 32 MiB of HBM per device.

```python
import math
import jax
import jax.numpy as jnp
from jax import lax

D = 6144
F = 24576
TOKENS = 2048
N_MP = 16


def block_levels(rng, shape, pieces, smallest, top_value):
    level, own = 1.0, jax.random.fold_in(rng, 6)
    for dim, blocks in pieces:
        heights = jnp.exp(jax.random.uniform(jax.random.fold_in(own, dim), (blocks,), jnp.float32, smallest / len(pieces), top_value / len(pieces)))
        level = level * jnp.repeat(heights, shape[dim] // blocks).reshape([-1 if axis == dim else 1 for axis in range(len(shape))])
    return level


def noise(rng, extent, deviation, bound, split=(), held_as=jnp.bfloat16):
    entries = jax.random.normal(rng, extent, jnp.float32) * deviation
    if len(split) > 0:
        entries = block_levels(rng, extent, split, -0.22, 0.18) * entries
    return jnp.clip(entries, min=-bound, max=bound).astype(held_as)


def setup_inputs(seed: int = 0) -> dict:
    splits = jax.random.split(jax.random.key(seed), 5)
    inputs = noise(splits[0], (TOKENS, D), 1.0, 6.0, ((0, 64), (1, 16)))
    act_grad = noise(splits[1], (TOKENS, F), 1.0, 6.0, ((0, 16), (1, 64)))
    w_in = noise(splits[2], (D, F), D ** -0.5, 0.078125, ((0, 16), (1, 64)))
    bias_in = noise(splits[3], (F,), 1.0, 5.0, ((0, 64),), jnp.float32)
    return {"inputs": inputs, "act_grad": act_grad, "w_in": w_in, "bias_in": bias_in}


def gelu_slope(pre):
    cdf = 0.5 * (1.0 + jax.scipy.special.erf(pre * (1.0 / math.sqrt(2.0))))
    dens = jnp.exp(-0.5 * pre * pre) * (1.0 / math.sqrt(2.0 * math.pi))
    return cdf + pre * dens

def reference(inputs, act_grad, w_in, bias_in):
    width = D // N_MP

    def add_group(total, group):
        start = (group * width).astype(jnp.int32)
        rows = lax.dynamic_slice_in_dim(inputs, start, width, 1)
        block = lax.dynamic_slice_in_dim(w_in, start, width, 0)
        part = jnp.dot(rows, block, preferred_element_type=jnp.float32).astype(jnp.bfloat16)
        return (total + part.astype(jnp.float32), None)
    total, _ = lax.scan(add_group, jnp.zeros((TOKENS, F), jnp.float32), jnp.arange(N_MP, dtype=jnp.int32))
    pre = total + bias_in
    hidden_grad = (act_grad.astype(jnp.float32) * gelu_slope(pre)).astype(jnp.bfloat16)
    w_in_grad = jnp.dot(inputs.T, hidden_grad, preferred_element_type=jnp.float32)
    bias_grad = lax.optimization_barrier(jnp.sum(hidden_grad.astype(jnp.float32), axis=0))
    input_grad = jnp.dot(hidden_grad, w_in.T, preferred_element_type=jnp.float32).astype(jnp.bfloat16)
    return (input_grad, w_in_grad, bias_grad)
```

```python
import functools
import math

import jax
import jax.numpy as jnp
from jax import lax
from jax.experimental import pallas as pl
from jax.experimental.pallas import tpu as pltpu
from jax.sharding import PartitionSpec as P

MESH = pl.DeviceIdType.MESH
F32, BF16 = jnp.float32, jnp.bfloat16
ROWS = 16


def gelu_slope(pre):
    cdf = 0.5 * (1.0 + lax.erf(pre * (1.0 / math.sqrt(2.0))))
    dens = jnp.exp(-0.5 * pre * pre) * (1.0 / math.sqrt(2.0 * math.pi))
    return cdf + pre * dens


def kernel(x_ref, a_ref, w_ref, b_ref, ig_ref, wg_ref, bg_ref,
           X, PA, RY, TY, Q, RZ, TZ, G, IG, RC, IX, RX, TX, K, RL, ssem, rsem):
    dp, mp = lax.axis_index("dp"), lax.axis_index("mp")
    zl, x, c = dp // 8, (dp // 2) % 4, dp % 2
    zh, y = mp // 4, mp % 4
    z0, zq, x1, x0 = zl % 2, zl // 2, x // 2, x % 2
    count = [0]
    sent = []

    def dev_zl(v):
        return (v * 8 + x * 2 + c, mp)

    def dev_x(v):
        return (zl * 8 + v * 2 + c, mp)

    def dev_y(v):
        return (dp, zh * 4 + v)

    def dev_z(v):
        return (dp, v * 4 + y)

    other = (zl * 8 + x * 2 + (1 - c), mp)

    def slot():
        count[0] += 1
        return count[0] - 1

    def send(src, dst, sem, dev):
        d = pltpu.make_async_remote_copy(
            src_ref=src, dst_ref=dst, send_sem=ssem.at[sem], recv_sem=rsem.at[sem],
            device_id=dev, device_id_type=MESH)
        d.start()
        sent.append(d)

    def landed(ref, sem):
        pltpu.make_async_remote_copy(
            src_ref=ref, dst_ref=ref, send_sem=ssem.at[sem], recv_sem=rsem.at[sem],
            device_id=other, device_id_type=MESH).wait_recv()

    def ag_start(me, dev, blk):
        up, down = (me + 1) % 4, (me + 3) % 4
        sems = [slot() for _ in range(6)]
        send(blk(me, 0), blk(me, 0), sems[0], dev(up))
        send(blk(me, 1), blk(me, 1), sems[3], dev(down))
        send(blk(me, 1), blk(me, 1), sems[1], dev(up))
        send(blk(me, 0), blk(me, 0), sems[4], dev(down))
        return sems

    def ag_forward(me, dev, blk, sems):
        up, down = (me + 1) % 4, (me + 3) % 4
        landed(blk(down, 0), sems[0])
        send(blk(down, 0), blk(down, 0), sems[2], dev(up))
        landed(blk(up, 1), sems[3])
        send(blk(up, 1), blk(up, 1), sems[5], dev(down))

    def ag_finish(me, blk, sems):
        up, down, far = (me + 1) % 4, (me + 3) % 4, (me + 2) % 4
        landed(blk(down, 1), sems[1])
        landed(blk(up, 0), sems[4])
        landed(blk(far, 0), sems[2])
        landed(blk(far, 1), sems[5])

    def rs_start(me, dev, blk, R):
        up, down, far = (me + 1) % 4, (me + 3) % 4, (me + 2) % 4
        sems = [slot() for _ in range(6)]
        send(blk(far, 0), R.at[0, 0], sems[0], dev(up))
        send(blk(far, 1), R.at[1, 0], sems[3], dev(down))
        send(blk(up, 1), R.at[0, 1], sems[1], dev(up))
        send(blk(down, 0), R.at[1, 1], sems[4], dev(down))
        return sems

    def rs_forward(me, dev, blk, R, T, sems):
        up, down = (me + 1) % 4, (me + 3) % 4
        landed(R.at[0, 0], sems[0])
        T[0] = (blk(up, 0)[...].astype(F32) + R[0, 0].astype(F32)).astype(BF16)
        send(T.at[0], R.at[0, 2], sems[2], dev(up))
        landed(R.at[1, 0], sems[3])
        T[1] = (blk(down, 1)[...].astype(F32) + R[1, 0].astype(F32)).astype(BF16)
        send(T.at[1], R.at[1, 2], sems[5], dev(down))

    def rs_finish(me, blk, R, sems):
        landed(R.at[1, 1], sems[4])
        landed(R.at[0, 1], sems[1])
        landed(R.at[0, 2], sems[2])
        landed(R.at[1, 2], sems[5])
        low = blk(me, 0)[...].astype(F32) + R[0, 2].astype(F32) + R[1, 1].astype(F32)
        high = blk(me, 1)[...].astype(F32) + R[1, 2].astype(F32) + R[0, 1].astype(F32)
        return low, high

    barrier = pltpu.get_barrier_semaphore()
    partners = [dev_zl((zl + d) % 8) for d in range(1, 8)]
    partners += [dev_x((x + 1) % 4), dev_x((x + 3) % 4)]
    partners += [dev_y((y + 1) % 4), dev_y((y + 3) % 4)]
    partners += [dev_z((zh + 1) % 4), dev_z((zh + 3) % 4), other]
    for p in partners:
        pl.semaphore_signal(barrier, inc=1, device_id=p, device_id_type=MESH)
    pl.semaphore_wait(barrier, len(partners))

    zsem = [slot() for _ in range(8)]
    for d in range(1, 8):
        send(x_ref, X.at[:, c, z0, x1, zq, x0], zsem[d], dev_zl((zl + d) % 8))
    X[:, c, z0, x1, zq, x0] = x_ref[...]
    for d in range(1, 8):
        s = (zl + 8 - d) % 8
        landed(X.at[:, c, s % 2, x1, s // 2, x0], zsem[d])

    def xblk(h):
        return lambda v, half: X.at[h, c, half, v // 2, :, v % 2]

    xs = [ag_start(x, dev_x, xblk(h)) for h in range(2)]
    for h in range(2):
        ag_forward(x, dev_x, xblk(h), xs[h])
    csem = [slot() for _ in range(2)]
    for h in range(2):
        ag_finish(x, xblk(h), xs[h])
        send(X.at[h, c], X.at[h, c], csem[h], other)

    def pblk(h):
        return lambda v, half: PA.at[h, half, v // 2, v % 2]

    ys = []
    for h in range(2):
        landed(X.at[h, 1 - c], csem[h])

        def pre_part(i, carry, h=h):
            rows = X[h, i // 2, i % 2].reshape(16 * ROWS, 384)
            part = jnp.dot(rows, w_ref[...], preferred_element_type=F32)
            PA[h, i // 2, i % 2] = part.astype(BF16).reshape(2, 4, 2, ROWS, 384)
            return carry

        lax.fori_loop(0, 4, pre_part, 0)
        ys.append(rs_start(y, dev_y, pblk(h), RY.at[h]))
    for h in range(2):
        rs_forward(y, dev_y, pblk(h), RY.at[h], TY.at[h], ys[h])

    def qblk(h):
        return lambda v, half: Q.at[h, half, v]

    zs = []
    for h in range(2):
        low, high = rs_finish(y, pblk(h), RY.at[h], ys[h])
        Q[h, 0] = low.astype(BF16)
        Q[h, 1] = high.astype(BF16)
        zs.append(rs_start(zh, dev_z, qblk(h), RZ.at[h]))
    for h in range(2):
        rs_forward(zh, dev_z, qblk(h), RZ.at[h], TZ.at[h], zs[h])

    def gz(h):
        return lambda v, half: G.at[h, half, y // 2, y % 2, v]

    def gy(h):
        return lambda v, half: G.at[h, half, v // 2, v % 2]

    gzs = []
    for h in range(2):
        sums = rs_finish(zh, qblk(h), RZ.at[h], zs[h])
        for half in range(2):
            for e in range(2):
                pre = sums[half][e] + b_ref[...]
                act = a_ref[pl.ds(32 * (2 * e + half) + ROWS * h, ROWS), :].astype(F32)
                G[h, half, y // 2, y % 2, zh, e] = (act * gelu_slope(pre)).astype(BF16)
        gzs.append(ag_start(zh, dev_z, gz(h)))
    for h in range(2):
        ag_forward(zh, dev_z, gz(h), gzs[h])
    gys = []
    for h in range(2):
        ag_finish(zh, gz(h), gzs[h])
        gys.append(ag_start(y, dev_y, gy(h)))
    for h in range(2):
        ag_forward(y, dev_y, gy(h), gys[h])

    isem = [slot() for _ in range(2)]
    for h in range(2):
        ag_finish(y, gy(h), gys[h])

        def ig_part(i, carry, h=h):
            rows = G[h, i // 2, i % 2].reshape(16 * ROWS, 384)
            part = lax.dot_general(rows, w_ref[...], (((1,), (1,)), ((), ())), preferred_element_type=F32)
            IG[h, i // 2, i % 2] = part.astype(BF16).reshape(2, 4, 2, ROWS, 384)
            return carry

        lax.fori_loop(0, 4, ig_part, 0)
        send(IG.at[h, 1 - c], RC.at[h], isem[h], other)

    def iblk(h):
        return lambda v, half: IX.at[h, half, v // 2, :, v % 2]

    ixs = []
    for h in range(2):
        landed(RC.at[h], isem[h])
        for half in range(2):
            IX[h, half] = (IG[h, c, half].astype(F32) + RC[h, half].astype(F32)).astype(BF16)
        ixs.append(rs_start(x, dev_x, iblk(h), RX.at[h]))
    for h in range(2):
        rs_forward(x, dev_x, iblk(h), RX.at[h], TX.at[h], ixs[h])
    lsems = []
    for h in range(2):
        low, high = rs_finish(x, iblk(h), RX.at[h], ixs[h])
        K[h, 0] = low.astype(BF16)
        K[h, 1] = high.astype(BF16)
        lsem = [slot() for _ in range(8)]
        lsems.append(lsem)
        for d in range(1, 8):
            t = (zl + d) % 8
            send(K.at[h, t % 2, t // 2], RL.at[h, d - 1], lsem[d], dev_zl(t))

    wg_ref[...] = jnp.zeros_like(wg_ref)
    bg_ref[...] = jnp.zeros_like(bg_ref)

    def wg_part(i, carry):
        h, j, k = i // 4, (i // 2) % 2, i % 2
        rows = G[h, j, k].reshape(16 * ROWS, 384)
        wg_ref[...] += lax.dot_general(
            X[h, j, k].reshape(16 * ROWS, 384), rows, (((0,), (0,)), ((), ())), preferred_element_type=F32)
        bg_ref[...] += jnp.sum(rows.astype(F32), axis=0, keepdims=True)
        return carry

    lax.fori_loop(0, 8, wg_part, 0)

    for h in range(2):
        total = K[h, z0, zq].astype(F32)
        for d in range(1, 8):
            landed(RL.at[h, d - 1], lsems[h][d])
            total = total + RL[h, d - 1].astype(F32)
        ig_ref[h] = total.astype(BF16)
    for d in sent:
        d.wait_send()


def body(inputs, act_grad, w_in, bias_in):
    vm = lambda *s: pltpu.VMEM(s, BF16)
    full = (2, 2, 2, 2, 4, 2, ROWS, 384)
    n = 140
    ig, wg, bg = pl.pallas_call(
        kernel,
        out_shape=(
            jax.ShapeDtypeStruct((2, ROWS, 384), BF16),
            jax.ShapeDtypeStruct((384, 384), F32),
            jax.ShapeDtypeStruct((1, 384), F32),
        ),
        in_specs=[pl.BlockSpec(memory_space=pltpu.VMEM)] * 4,
        out_specs=[pl.BlockSpec(memory_space=pltpu.VMEM)] * 3,
        scratch_shapes=[
            vm(*full),
            vm(*full),
            vm(2, 2, 3, 4, 2, ROWS, 384),
            vm(2, 2, 4, 2, ROWS, 384),
            vm(2, 2, 4, 2, ROWS, 384),
            vm(2, 2, 3, 2, ROWS, 384),
            vm(2, 2, 2, ROWS, 384),
            vm(*full),
            vm(*full),
            vm(2, 2, 2, 4, 2, ROWS, 384),
            vm(2, 2, 2, 4, 2, ROWS, 384),
            vm(2, 2, 3, 4, ROWS, 384),
            vm(2, 2, 4, ROWS, 384),
            vm(2, 2, 4, ROWS, 384),
            vm(2, 7, ROWS, 384),
            pltpu.SemaphoreType.DMA((n,)),
            pltpu.SemaphoreType.DMA((n,)),
        ],
        compiler_params=pltpu.CompilerParams(
            collective_id=0, has_side_effects=True, vmem_limit_bytes=48 * 1024 * 1024
        ),
    )(inputs.reshape(2, ROWS, 384), act_grad, w_in, bias_in.reshape(1, 384))
    return (ig.reshape(2 * ROWS, 384), wg, bg.reshape(384))


def solution(mesh):
    return jax.shard_map(
        body,
        mesh=mesh,
        in_specs=(P("dp", "mp"), P("mp", "dp"), P("mp", "dp"), P("dp")),
        out_specs=(P("dp", "mp"), P("mp", "dp"), P("dp")),
        check_vma=False,
    )
```

```python
import math

import jax
import jax.numpy as jnp
from jax import lax
from jax.experimental import pallas as pl
from jax.experimental.pallas import tpu as pltpu
from jax.sharding import PartitionSpec as P

MESH = pl.DeviceIdType.MESH
F32, BF16 = jnp.float32, jnp.bfloat16
ROWS = 16
CHUNKS = tuple((h, a, e) for h in range(2) for a in range(2) for e in range(2))
ORDER = (
    "zw0 zw1 xa0 b0 b1 xb0 b2 xa1 b3 b4 d0 xb1 b5 d1 b7 d2 b6 d3 d4 e0 d5 e1 d7 e2 d6 e3 e4 f0 e5 f1 e7 f2 f3 e6 f4 g0 f5 g1 g2 f7 g3 f6 g4 h0 g5 h1 h2 g7 j0 w0 h3 j1 w1 g6 j2 l0 h5 h4 w2 j3 h7 w3 l1 j5 h6 w5 j4 l2 w4 j7 n0 j6 l3 w6 w7 n1 o0 o1"
).split()


def gelu_slope(pre):
    cdf = 0.5 * (1.0 + lax.erf(pre * (1.0 / math.sqrt(2.0))))
    dens = jnp.exp(-0.5 * pre * pre) * (1.0 / math.sqrt(2.0 * math.pi))
    return cdf + pre * dens


def kernel(x_hbm, a_hbm, w_hbm, b_hbm, ig_ref, wg_ref, bg_ref,
           A, W, B, X, PA, RY, Q, RZ, TZ, G, IG, RC, IX, RX, K, RL, BG, lsem, ssem, rsem):
    dp, mp = lax.axis_index("dp"), lax.axis_index("mp")
    zl, x, c = dp // 8, (dp // 2) % 4, dp % 2
    zh, y = mp // 4, mp % 4
    z0, zq, x1, x0 = zl % 2, zl // 2, x // 2, x % 2
    count = [0]
    sent = []

    def dev_zl(v):
        return (v * 8 + x * 2 + c, mp)

    def dev_x(v):
        return (zl * 8 + v * 2 + c, mp)

    def dev_y(v):
        return (dp, zh * 4 + v)

    def dev_z(v):
        return (dp, v * 4 + y)

    other = (zl * 8 + x * 2 + (1 - c), mp)

    def slots(k):
        count[0] += k
        return list(range(count[0] - k, count[0]))

    def send(src, dst, sem, dev):
        d = pltpu.make_async_remote_copy(
            src_ref=src, dst_ref=dst, send_sem=ssem.at[sem], recv_sem=rsem.at[sem],
            device_id=dev, device_id_type=MESH)
        d.start()
        sent.append(d)

    def landed(ref, sem):
        pltpu.make_async_remote_copy(
            src_ref=ref, dst_ref=ref, send_sem=ssem.at[sem], recv_sem=rsem.at[sem],
            device_id=other, device_id_type=MESH).wait_recv()

    own = [
        pltpu.make_async_copy(w_hbm, W, lsem.at[0]),
        pltpu.make_async_copy(a_hbm, A, lsem.at[1]),
        pltpu.make_async_copy(b_hbm, B, lsem.at[2]),
    ]
    own += [
        pltpu.make_async_copy(
            x_hbm.at[pl.ds(h * ROWS, ROWS)], X.at[h, c, x0, z0, x1, zq], lsem.at[3 + h])
        for h in range(2)
    ]
    for d in own:
        d.start()

    barrier = pltpu.get_barrier_semaphore()
    partners = [dev_zl((zl + d) % 8) for d in range(1, 8)]
    partners += [dev_x((x + d) % 4) for d in range(1, 4)]
    partners += [dev_y((y + d) % 4) for d in range(1, 4)]
    partners += [dev_z((zh + 1) % 4), dev_z((zh + 3) % 4), other]
    for p in partners:
        pl.semaphore_signal(barrier, inc=1, device_id=p, device_id_type=MESH)
    for d in own:
        d.wait()
    pl.semaphore_wait(barrier, len(partners))

    s_in, s_x, s_core = [slots(8) for _ in range(2)], [slots(4) for _ in range(2)], [slots(2) for _ in range(2)]
    s_y, s_z = [slots(4) for _ in CHUNKS], [slots(3) for _ in CHUNKS]
    s_gz, s_gy = [slots(3) for _ in CHUNKS], [slots(4) for _ in CHUNKS]
    s_ic, s_ix, s_out = [slots(2) for _ in range(2)], [slots(4) for _ in range(2)], [slots(8) for _ in range(2)]

    def tok(q):
        h, a, e = CHUNKS[q]
        return h, (c if e == 0 else 1 - c), (x0 if a == 0 else 1 - x0)

    def ways(q):
        up, down = (zh + 1) % 4, (zh + 3) % 4
        return (up, down) if q % 2 == 0 else (down, up)

    def zw(h):
        for d in range(1, 8):
            s = (zl + 8 - d) % 8
            landed(X.at[h, c, x0, s % 2, x1, s // 2], s_in[h][d])
        mine = X.at[h, c, x0, :, x1]
        for d in (2, 1, 3):
            send(mine, mine, s_x[h][d], dev_x((x + d) % 4))

    def from_x(h, d):
        s = (x + 4 - d) % 4
        landed(X.at[h, c, s % 2, :, s // 2], s_x[h][d])

    def xa(h):
        from_x(h, 2)
        send(X.at[h, c, x0], X.at[h, c, x0], s_core[h][0], other)

    def xb(h):
        from_x(h, 1)
        from_x(h, 3)
        send(X.at[h, c, 1 - x0], X.at[h, c, 1 - x0], s_core[h][1], other)

    def b(q):
        h, t, s = tok(q)
        if CHUNKS[q][2] == 1:
            landed(X.at[h, t, s], s_core[h][CHUNKS[q][1]])
        out = jnp.dot(X[h, t, s].reshape(16 * ROWS, 384), W[...], preferred_element_type=F32)
        PA[q] = out.astype(BF16).reshape(4, 4, ROWS, 384)
        for d in (2, 1, 3):
            v = (y + d) % 4
            send(PA.at[q, v], RY.at[q, d - 1], s_y[q][d], dev_y(v))

    def d_(q):
        total = PA[q, y].astype(F32)
        for d in range(1, 4):
            landed(RY.at[q, d - 1], s_y[q][d])
            total = total + RY[q, d - 1].astype(F32)
        Q[q] = total.astype(BF16)
        first, second = ways(q)
        send(Q.at[q, (zh + 2) % 4], RZ.at[q, 0], s_z[q][0], dev_z(first))
        send(Q.at[q, second], RZ.at[q, 1], s_z[q][1], dev_z(second))

    def e_(q):
        first, second = ways(q)
        landed(RZ.at[q, 0], s_z[q][0])
        TZ[q] = (Q[q, first].astype(F32) + RZ[q, 0].astype(F32)).astype(BF16)
        send(TZ.at[q], RZ.at[q, 2], s_z[q][2], dev_z(first))

    def f_(q):
        h, t, s = tok(q)
        landed(RZ.at[q, 1], s_z[q][1])
        landed(RZ.at[q, 2], s_z[q][2])
        pre = Q[q, zh].astype(F32) + RZ[q, 1].astype(F32) + RZ[q, 2].astype(F32) + B[...].reshape(1, 384)
        row = pl.multiple_of(64 * s + 32 * t + ROWS * h, ROWS)
        act = A[pl.ds(row, ROWS), :].astype(F32)
        G[q, y, zh] = (act * gelu_slope(pre)).astype(BF16)
        first, second = ways(q)
        mine = G.at[q, y, zh]
        send(mine, mine, s_gz[q][0], dev_z(first))
        send(mine, mine, s_gz[q][1], dev_z(second))

    def g_(q):
        first, second = ways(q)
        landed(G.at[q, y, second], s_gz[q][0])
        send(G.at[q, y, second], G.at[q, y, second], s_gz[q][2], dev_z(first))

    def h_(q):
        first, second = ways(q)
        landed(G.at[q, y, first], s_gz[q][1])
        landed(G.at[q, y, (zh + 2) % 4], s_gz[q][2])
        for d in (2, 1, 3):
            send(G.at[q, y], G.at[q, y], s_gy[q][d], dev_y((y + d) % 4))

    def j_(q):
        h, a, e = CHUNKS[q]
        for d in range(1, 4):
            landed(G.at[q, (y + 4 - d) % 4], s_gy[q][d])
        out = lax.dot_general(
            G[q].reshape(16 * ROWS, 384), W[...], (((1,), (1,)), ((), ())), preferred_element_type=F32)
        IG[q] = out.astype(BF16).reshape(2, 2, 4, ROWS, 384)
        if e == 1:
            send(IG.at[q], RC.at[h, a], s_ic[h][a], other)

    def l_(k):
        h, a = k // 2, k % 2
        landed(RC.at[h, a], s_ic[h][a])
        both = IG[CHUNKS.index((h, a, 0))].astype(F32) + RC[h, a].astype(F32)
        for i in range(2):
            IX[h, a, i] = both[:, i].astype(BF16)
        for d in ((2,) if a == 0 else (1, 3)):
            v = (x + d) % 4
            send(IX.at[h, a, v // 2], RX.at[h, d - 1], s_ix[h][d], dev_x(v))

    def n_(h):
        total = IX[h, 0, x1].astype(F32)
        for d in range(1, 4):
            landed(RX.at[h, d - 1], s_ix[h][d])
            total = total + RX[h, d - 1].astype(F32)
        K[h] = total.astype(BF16)
        for d in range(1, 8):
            t = (zl + d) % 8
            send(K.at[h, t % 2, t // 2], RL.at[h, d - 1], s_out[h][d], dev_zl(t))

    def o_(h):
        total = K[h, z0, zq].astype(F32)
        for d in range(1, 8):
            landed(RL.at[h, d - 1], s_out[h][d])
            total = total + RL[h, d - 1].astype(F32)
        ig_ref[pl.ds(h * ROWS, ROWS), :] = total.astype(BF16)

    def w_(q):
        h, t, s = tok(q)
        rows = G[q].reshape(16 * ROWS, 384)
        wg_ref[...] += lax.dot_general(
            X[h, t, s].reshape(16 * ROWS, 384), rows, (((0,), (0,)), ((), ())), preferred_element_type=F32)
        BG[...] += jnp.sum(rows.astype(F32), axis=0, keepdims=True)

    for h in range(2):
        for d in range(1, 8):
            send(x_hbm.at[pl.ds(h * ROWS, ROWS)], X.at[h, c, x0, z0, x1, zq], s_in[h][d], dev_zl((zl + d) % 8))
    wg_ref[...] = jnp.zeros_like(wg_ref)
    BG[...] = jnp.zeros_like(BG)
    tasks = {"zw": zw, "xa": xa, "xb": xb, "b": b, "d": d_, "e": e_, "f": f_, "g": g_, "h": h_,
             "j": j_, "l": l_, "n": n_, "o": o_, "w": w_}
    for task in ORDER:
        tasks[task[:-1]](int(task[-1]))
    bg_ref[...] = BG[...].reshape(384)
    for d in sent:
        d.wait_send()


def body(inputs, act_grad, w_in, bias_in):
    vm = lambda *s: pltpu.VMEM(s, BF16)
    nq, n = len(CHUNKS), 180
    return pl.pallas_call(
        kernel,
        out_shape=(
            jax.ShapeDtypeStruct((2 * ROWS, 384), BF16),
            jax.ShapeDtypeStruct((384, 384), F32),
            jax.ShapeDtypeStruct((384,), F32),
        ),
        in_specs=[pl.BlockSpec(memory_space=pl.ANY)] * 4,
        out_specs=[pl.BlockSpec(memory_space=pltpu.VMEM)] * 3,
        scratch_shapes=[
            vm(128, 384),
            vm(384, 384),
            pltpu.VMEM((384,), F32),
            vm(2, 2, 2, 2, 2, 4, ROWS, 384),
            vm(nq, 4, 4, ROWS, 384),
            vm(nq, 3, 4, ROWS, 384),
            vm(nq, 4, ROWS, 384),
            vm(nq, 3, ROWS, 384),
            vm(nq, ROWS, 384),
            vm(nq, 4, 4, ROWS, 384),
            vm(nq, 2, 2, 4, ROWS, 384),
            vm(2, 2, 2, 2, 4, ROWS, 384),
            vm(2, 2, 2, 2, 4, ROWS, 384),
            vm(2, 3, 2, 4, ROWS, 384),
            vm(2, 2, 4, ROWS, 384),
            vm(2, 7, ROWS, 384),
            pltpu.VMEM((1, 384), F32),
            pltpu.SemaphoreType.DMA((5,)),
            pltpu.SemaphoreType.DMA((n,)),
            pltpu.SemaphoreType.DMA((n,)),
        ],
        compiler_params=pltpu.CompilerParams(
            collective_id=0, has_side_effects=True, vmem_limit_bytes=56 * 1024 * 1024
        ),
    )(inputs, act_grad, w_in, bias_in)


def solution(mesh):
    return jax.shard_map(
        body,
        mesh=mesh,
        in_specs=(P("dp", "mp"), P("mp", "dp"), P("mp", "dp"), P("dp")),
        out_specs=(P("dp", "mp"), P("mp", "dp"), P("dp")),
        check_vma=False,
    )
```

```python
import math

import jax
import jax.numpy as jnp
from jax import lax
from jax.experimental import pallas as pl
from jax.experimental.pallas import tpu as pltpu
from jax.sharding import PartitionSpec as P

MESH = pl.DeviceIdType.MESH
F32, BF16 = jnp.float32, jnp.bfloat16
ROWS = 16
CHUNKS = tuple((h, a, e) for h in range(2) for a in range(2) for e in range(2))
ORDER = (
    "zw0 zs1 xa0 b0 zw1 b1 xb0 b2 xa1 b4 d0 xb1 b5 d1 b3 d2 b6 d4 b7 e0 d5 d3 e1 d6 e2 d7 f0 e3 f1 e7 e5 f2 e6 g0 f3 g1 f7 e4 h0 f5 g3 f6 g2 h1 g7 f4 j1 g6 g5 h3 w1 h2 j0 w0 g4 h7 j3 h6 j2 h5 w2 j7 l1 h4 l0 w3 j6 l3 j5 w5 j4 l2 n0 w6 w7 n1 w4 o0 o1"
).split()


def gelu_slope(pre):
    cdf = 0.5 * (1.0 + lax.erf(pre * (1.0 / math.sqrt(2.0))))
    dens = jnp.exp(-0.5 * pre * pre) * (1.0 / math.sqrt(2.0 * math.pi))
    return cdf + pre * dens


def kernel(x_hbm, a_hbm, w_hbm, b_hbm, ig_ref, wg_ref, bg_ref,
           A, W, B, X, PA, RY, Q, RZ, TZ, G, IG, RC, IX, RX, K, RL, BG, lsem, ssem, rsem):
    dp, mp = lax.axis_index("dp"), lax.axis_index("mp")
    zl, x, c = dp // 8, (dp // 2) % 4, dp % 2
    zh, y = mp // 4, mp % 4
    z0, zq, x1, x0 = zl % 2, zl // 2, x // 2, x % 2
    count = [0]
    sent = []

    def dev_zl(v):
        return (v * 8 + x * 2 + c, mp)

    def dev_x(v):
        return (zl * 8 + v * 2 + c, mp)

    def dev_y(v):
        return (dp, zh * 4 + v)

    def dev_z(v):
        return (dp, v * 4 + y)

    other = (zl * 8 + x * 2 + (1 - c), mp)

    def slots(k):
        count[0] += k
        return list(range(count[0] - k, count[0]))

    def send(src, dst, sem, dev):
        d = pltpu.make_async_remote_copy(
            src_ref=src, dst_ref=dst, send_sem=ssem.at[sem], recv_sem=rsem.at[sem],
            device_id=dev, device_id_type=MESH)
        d.start()
        sent.append(d)

    def landed(ref, sem):
        pltpu.make_async_remote_copy(
            src_ref=ref, dst_ref=ref, send_sem=ssem.at[sem], recv_sem=rsem.at[sem],
            device_id=other, device_id_type=MESH).wait_recv()

    own = [
        pltpu.make_async_copy(w_hbm, W, lsem.at[0]),
        pltpu.make_async_copy(a_hbm, A, lsem.at[1]),
        pltpu.make_async_copy(b_hbm, B, lsem.at[2]),
    ]
    own += [
        pltpu.make_async_copy(
            x_hbm.at[pl.ds(h * ROWS, ROWS)], X.at[h, c, x0, z0, x1, zq], lsem.at[3 + h])
        for h in range(2)
    ]
    for d in own:
        d.start()

    barrier = pltpu.get_barrier_semaphore()
    partners = [dev_zl((zl + d) % 8) for d in range(1, 8)]
    partners += [dev_x((x + d) % 4) for d in range(1, 4)]
    partners += [dev_y((y + d) % 4) for d in range(1, 4)]
    partners += [dev_z((zh + 1) % 4), dev_z((zh + 3) % 4), other]
    for p in partners:
        pl.semaphore_signal(barrier, inc=1, device_id=p, device_id_type=MESH)
    for d in own:
        d.wait()
    pl.semaphore_wait(barrier, len(partners))

    s_in, s_x, s_core = [slots(8) for _ in range(2)], [slots(4) for _ in range(2)], [slots(2) for _ in range(2)]
    s_y, s_z = [slots(4) for _ in CHUNKS], [slots(3) for _ in CHUNKS]
    s_gz, s_gy = [slots(3) for _ in CHUNKS], [slots(4) for _ in CHUNKS]
    s_ic, s_ix, s_out = [slots(2) for _ in range(2)], [slots(4) for _ in range(2)], [slots(8) for _ in range(2)]

    def tok(q):
        h, a, e = CHUNKS[q]
        return h, (c if e == 0 else 1 - c), (x0 if a == 0 else 1 - x0)

    def ways(q):
        up, down = (zh + 1) % 4, (zh + 3) % 4
        return (up, down) if q % 2 == 0 else (down, up)

    def zw(h):
        for d in range(1, 8):
            s = (zl + 8 - d) % 8
            landed(X.at[h, c, x0, s % 2, x1, s // 2], s_in[h][d])
        mine = X.at[h, c, x0, :, x1]
        for d in (2, 1, 3):
            send(mine, mine, s_x[h][d], dev_x((x + d) % 4))

    def from_x(h, d):
        s = (x + 4 - d) % 4
        landed(X.at[h, c, s % 2, :, s // 2], s_x[h][d])

    def xa(h):
        from_x(h, 2)
        send(X.at[h, c, x0], X.at[h, c, x0], s_core[h][0], other)

    def xb(h):
        from_x(h, 1)
        from_x(h, 3)
        send(X.at[h, c, 1 - x0], X.at[h, c, 1 - x0], s_core[h][1], other)

    def b(q):
        h, t, s = tok(q)
        if CHUNKS[q][2] == 1:
            landed(X.at[h, t, s], s_core[h][CHUNKS[q][1]])
        out = jnp.dot(X[h, t, s].reshape(16 * ROWS, 384), W[...], preferred_element_type=F32)
        PA[q] = out.astype(BF16).reshape(4, 4, ROWS, 384)
        for d in (2, 1, 3):
            v = (y + d) % 4
            send(PA.at[q, v], RY.at[q, d - 1], s_y[q][d], dev_y(v))

    def d_(q):
        total = PA[q, y].astype(F32)
        for d in range(1, 4):
            landed(RY.at[q, d - 1], s_y[q][d])
            total = total + RY[q, d - 1].astype(F32)
        Q[q] = total.astype(BF16)
        first, second = ways(q)
        send(Q.at[q, (zh + 2) % 4], RZ.at[q, 0], s_z[q][0], dev_z(first))
        send(Q.at[q, second], RZ.at[q, 1], s_z[q][1], dev_z(second))

    def e_(q):
        first, second = ways(q)
        landed(RZ.at[q, 0], s_z[q][0])
        TZ[q] = (Q[q, first].astype(F32) + RZ[q, 0].astype(F32)).astype(BF16)
        send(TZ.at[q], RZ.at[q, 2], s_z[q][2], dev_z(first))

    def f_(q):
        h, t, s = tok(q)
        landed(RZ.at[q, 1], s_z[q][1])
        landed(RZ.at[q, 2], s_z[q][2])
        pre = Q[q, zh].astype(F32) + RZ[q, 1].astype(F32) + RZ[q, 2].astype(F32) + B[...].reshape(1, 384)
        row = pl.multiple_of(64 * s + 32 * t + ROWS * h, ROWS)
        act = A[pl.ds(row, ROWS), :].astype(F32)
        G[q, y, zh] = (act * gelu_slope(pre)).astype(BF16)
        first, second = ways(q)
        mine = G.at[q, y, zh]
        send(mine, mine, s_gz[q][0], dev_z(first))
        send(mine, mine, s_gz[q][1], dev_z(second))

    def g_(q):
        first, second = ways(q)
        landed(G.at[q, y, second], s_gz[q][0])
        send(G.at[q, y, second], G.at[q, y, second], s_gz[q][2], dev_z(first))

    def h_(q):
        first, second = ways(q)
        landed(G.at[q, y, first], s_gz[q][1])
        landed(G.at[q, y, (zh + 2) % 4], s_gz[q][2])
        for d in (2, 1, 3):
            send(G.at[q, y], G.at[q, y], s_gy[q][d], dev_y((y + d) % 4))

    def j_(q):
        h, a, e = CHUNKS[q]
        for d in range(1, 4):
            landed(G.at[q, (y + 4 - d) % 4], s_gy[q][d])
        out = lax.dot_general(
            G[q].reshape(16 * ROWS, 384), W[...], (((1,), (1,)), ((), ())), preferred_element_type=F32)
        IG[q] = out.astype(BF16).reshape(2, 2, 4, ROWS, 384)
        if e == 1:
            send(IG.at[q], RC.at[h, a], s_ic[h][a], other)

    def l_(k):
        h, a = k // 2, k % 2
        landed(RC.at[h, a], s_ic[h][a])
        both = IG[CHUNKS.index((h, a, 0))].astype(F32) + RC[h, a].astype(F32)
        for i in range(2):
            IX[h, a, i] = both[:, i].astype(BF16)
        for d in ((2,) if a == 0 else (1, 3)):
            v = (x + d) % 4
            send(IX.at[h, a, v // 2], RX.at[h, d - 1], s_ix[h][d], dev_x(v))

    def n_(h):
        total = IX[h, 0, x1].astype(F32)
        for d in range(1, 4):
            landed(RX.at[h, d - 1], s_ix[h][d])
            total = total + RX[h, d - 1].astype(F32)
        K[h] = total.astype(BF16)
        for d in range(1, 8):
            t = (zl + d) % 8
            send(K.at[h, t % 2, t // 2], RL.at[h, d - 1], s_out[h][d], dev_zl(t))

    def o_(h):
        total = K[h, z0, zq].astype(F32)
        for d in range(1, 8):
            landed(RL.at[h, d - 1], s_out[h][d])
            total = total + RL[h, d - 1].astype(F32)
        ig_ref[pl.ds(h * ROWS, ROWS), :] = total.astype(BF16)

    def w_(q):
        h, t, s = tok(q)
        rows = G[q].reshape(16 * ROWS, 384)
        wg_ref[...] += lax.dot_general(
            X[h, t, s].reshape(16 * ROWS, 384), rows, (((0,), (0,)), ((), ())), preferred_element_type=F32)
        BG[...] += jnp.sum(rows.astype(F32), axis=0, keepdims=True)

    def zs(h):
        for d in range(1, 8):
            send(x_hbm.at[pl.ds(h * ROWS, ROWS)], X.at[h, c, x0, z0, x1, zq], s_in[h][d], dev_zl((zl + d) % 8))

    zs(0)
    wg_ref[...] = jnp.zeros_like(wg_ref)
    BG[...] = jnp.zeros_like(BG)
    tasks = {"zs": zs, "zw": zw, "xa": xa, "xb": xb, "b": b, "d": d_, "e": e_, "f": f_, "g": g_, "h": h_,
             "j": j_, "l": l_, "n": n_, "o": o_, "w": w_}
    for task in ORDER[:-1]:
        tasks[task[:-1]](int(task[-1]))
    bg_ref[...] = BG[...].reshape(384)
    for d in sent:
        d.wait_send()
    tasks[ORDER[-1][:-1]](int(ORDER[-1][-1]))


def body(inputs, act_grad, w_in, bias_in):
    vm = lambda *s: pltpu.VMEM(s, BF16)
    nq, n = len(CHUNKS), 180
    return pl.pallas_call(
        kernel,
        out_shape=(
            jax.ShapeDtypeStruct((2 * ROWS, 384), BF16),
            jax.ShapeDtypeStruct((384, 384), F32),
            jax.ShapeDtypeStruct((384,), F32),
        ),
        in_specs=[pl.BlockSpec(memory_space=pl.ANY)] * 4,
        out_specs=[pl.BlockSpec(memory_space=pltpu.VMEM)] * 3,
        scratch_shapes=[
            vm(128, 384),
            vm(384, 384),
            pltpu.VMEM((384,), F32),
            vm(2, 2, 2, 2, 2, 4, ROWS, 384),
            vm(nq, 4, 4, ROWS, 384),
            vm(nq, 3, 4, ROWS, 384),
            vm(nq, 4, ROWS, 384),
            vm(nq, 3, ROWS, 384),
            vm(nq, ROWS, 384),
            vm(nq, 4, 4, ROWS, 384),
            vm(nq, 2, 2, 4, ROWS, 384),
            vm(2, 2, 2, 2, 4, ROWS, 384),
            vm(2, 2, 2, 2, 4, ROWS, 384),
            vm(2, 3, 2, 4, ROWS, 384),
            vm(2, 2, 4, ROWS, 384),
            vm(2, 7, ROWS, 384),
            pltpu.VMEM((1, 384), F32),
            pltpu.SemaphoreType.DMA((5,)),
            pltpu.SemaphoreType.DMA((n,)),
            pltpu.SemaphoreType.DMA((n,)),
        ],
        compiler_params=pltpu.CompilerParams(
            collective_id=0, has_side_effects=True, vmem_limit_bytes=56 * 1024 * 1024
        ),
    )(inputs, act_grad, w_in, bias_in)


def solution(mesh):
    return jax.shard_map(
        body,
        mesh=mesh,
        in_specs=(P("dp", "mp"), P("mp", "dp"), P("mp", "dp"), P("dp")),
        out_specs=(P("dp", "mp"), P("mp", "dp"), P("dp")),
        check_vma=False,
    )
```

```python
import math

import jax
import jax.numpy as jnp
from jax import lax
from jax.experimental import pallas as pl
from jax.experimental.pallas import tpu as pltpu
from jax.sharding import PartitionSpec as P

MESH = pl.DeviceIdType.MESH
F32, BF16 = jnp.float32, jnp.bfloat16
ROWS = 16
CHUNKS = tuple((h, a, e) for h in range(2) for a in range(2) for e in range(2))
ORDER = (
    "zw0 zs1 xa0 b0 zw1 b1 xa1 b4 xb0 b2 d0 xb1 b5 d1 b3 d2 b6 d4 b7 e0 d5 d3 e1 d6 e2 d7 f0 e3 f1 e7 e5 f2 e6 g0 f3 g1 f7 e4 h0 f5 g3 f6 g2 h1 g7 f4 j1 g6 g5 h3 w1 h2 j0 l0 w0 g4 h7 j3 h6 j2 l1 h5 w2 j7 h4 n0 j6 l3 j5 j4 l2 n1 w3 w5 w6 w7 w4 o0 o1"
).split()


def gelu_slope(pre):
    cdf = 0.5 * (1.0 + lax.erf(pre * (1.0 / math.sqrt(2.0))))
    dens = jnp.exp(-0.5 * pre * pre) * (1.0 / math.sqrt(2.0 * math.pi))
    return cdf + pre * dens


def kernel(x_hbm, a_hbm, w_hbm, b_hbm, ig_ref, wg_ref, bg_ref,
           A, W, B, X, PA, RY, Q, RZ, TZ, G, IG, RC, IX, RX, K, RL, BG, lsem, ssem, rsem):
    dp, mp = lax.axis_index("dp"), lax.axis_index("mp")
    zl, x, c = dp // 8, (dp // 2) % 4, dp % 2
    zh, y = mp // 4, mp % 4
    z0, zq, x1, x0 = zl % 2, zl // 2, x // 2, x % 2
    count = [0]
    sent = []

    def dev_zl(v):
        return (v * 8 + x * 2 + c, mp)

    def dev_x(v):
        return (zl * 8 + v * 2 + c, mp)

    def dev_y(v):
        return (dp, zh * 4 + v)

    def dev_z(v):
        return (dp, v * 4 + y)

    other = (zl * 8 + x * 2 + (1 - c), mp)

    def slots(k):
        count[0] += k
        return list(range(count[0] - k, count[0]))

    def send(src, dst, sem, dev):
        d = pltpu.make_async_remote_copy(
            src_ref=src, dst_ref=dst, send_sem=ssem.at[sem], recv_sem=rsem.at[sem],
            device_id=dev, device_id_type=MESH)
        d.start()
        sent.append(d)

    def landed(ref, sem):
        pltpu.make_async_remote_copy(
            src_ref=ref, dst_ref=ref, send_sem=ssem.at[sem], recv_sem=rsem.at[sem],
            device_id=other, device_id_type=MESH).wait_recv()

    own = [
        pltpu.make_async_copy(w_hbm, W, lsem.at[0]),
        pltpu.make_async_copy(a_hbm, A, lsem.at[1]),
        pltpu.make_async_copy(b_hbm, B, lsem.at[2]),
    ]
    own += [
        pltpu.make_async_copy(
            x_hbm.at[pl.ds(h * ROWS, ROWS)], X.at[h, c, x0, z0, x1, zq], lsem.at[3 + h])
        for h in range(2)
    ]
    for d in own:
        d.start()

    barrier = pltpu.get_barrier_semaphore()
    partners = [dev_zl((zl + d) % 8) for d in range(1, 8)]
    partners += [dev_x((x + d) % 4) for d in range(1, 4)]
    partners += [dev_y((y + d) % 4) for d in range(1, 4)]
    partners += [dev_z((zh + 1) % 4), dev_z((zh + 3) % 4), other]
    for p in partners:
        pl.semaphore_signal(barrier, inc=1, device_id=p, device_id_type=MESH)
    for d in own:
        d.wait()
    pl.semaphore_wait(barrier, len(partners))

    s_in, s_x, s_core = [slots(8) for _ in range(2)], [slots(4) for _ in range(2)], [slots(2) for _ in range(2)]
    s_y, s_z = [slots(4) for _ in CHUNKS], [slots(3) for _ in CHUNKS]
    s_gz, s_gy = [slots(3) for _ in CHUNKS], [slots(4) for _ in CHUNKS]
    s_ic, s_ix, s_out = [slots(2) for _ in range(2)], [slots(4) for _ in range(2)], [slots(8) for _ in range(2)]

    def tok(q):
        h, a, e = CHUNKS[q]
        return h, (c if e == 0 else 1 - c), (x0 if a == 0 else 1 - x0)

    def ways(q):
        up, down = (zh + 1) % 4, (zh + 3) % 4
        return (up, down) if q % 2 == 0 else (down, up)

    def zw(h):
        for d in range(1, 8):
            s = (zl + 8 - d) % 8
            landed(X.at[h, c, x0, s % 2, x1, s // 2], s_in[h][d])
        mine = X.at[h, c, x0, :, x1]
        for d in (2, 1, 3):
            send(mine, mine, s_x[h][d], dev_x((x + d) % 4))

    def from_x(h, d):
        s = (x + 4 - d) % 4
        landed(X.at[h, c, s % 2, :, s // 2], s_x[h][d])

    def xa(h):
        from_x(h, 2)
        send(X.at[h, c, x0], X.at[h, c, x0], s_core[h][0], other)

    def xb(h):
        from_x(h, 1)
        from_x(h, 3)
        send(X.at[h, c, 1 - x0], X.at[h, c, 1 - x0], s_core[h][1], other)

    def b(q):
        h, t, s = tok(q)
        if CHUNKS[q][2] == 1:
            landed(X.at[h, t, s], s_core[h][CHUNKS[q][1]])
        out = jnp.dot(X[h, t, s].reshape(16 * ROWS, 384), W[...], preferred_element_type=F32)
        PA[q] = out.astype(BF16).reshape(4, 4, ROWS, 384)
        for d in (2, 1, 3):
            v = (y + d) % 4
            send(PA.at[q, v], RY.at[q, d - 1], s_y[q][d], dev_y(v))

    def d_(q):
        total = PA[q, y].astype(F32)
        for d in range(1, 4):
            landed(RY.at[q, d - 1], s_y[q][d])
            total = total + RY[q, d - 1].astype(F32)
        Q[q] = total.astype(BF16)
        first, second = ways(q)
        send(Q.at[q, (zh + 2) % 4], RZ.at[q, 0], s_z[q][0], dev_z(first))
        send(Q.at[q, second], RZ.at[q, 1], s_z[q][1], dev_z(second))

    def e_(q):
        first, second = ways(q)
        landed(RZ.at[q, 0], s_z[q][0])
        TZ[q] = (Q[q, first].astype(F32) + RZ[q, 0].astype(F32)).astype(BF16)
        send(TZ.at[q], RZ.at[q, 2], s_z[q][2], dev_z(first))

    def f_(q):
        h, t, s = tok(q)
        landed(RZ.at[q, 1], s_z[q][1])
        landed(RZ.at[q, 2], s_z[q][2])
        pre = Q[q, zh].astype(F32) + RZ[q, 1].astype(F32) + RZ[q, 2].astype(F32) + B[...].reshape(1, 384)
        row = pl.multiple_of(64 * s + 32 * t + ROWS * h, ROWS)
        act = A[pl.ds(row, ROWS), :].astype(F32)
        G[q, y, zh] = (act * gelu_slope(pre)).astype(BF16)
        first, second = ways(q)
        mine = G.at[q, y, zh]
        send(mine, mine, s_gz[q][0], dev_z(first))
        send(mine, mine, s_gz[q][1], dev_z(second))

    def g_(q):
        first, second = ways(q)
        landed(G.at[q, y, second], s_gz[q][0])
        send(G.at[q, y, second], G.at[q, y, second], s_gz[q][2], dev_z(first))

    def h_(q):
        first, second = ways(q)
        landed(G.at[q, y, first], s_gz[q][1])
        landed(G.at[q, y, (zh + 2) % 4], s_gz[q][2])
        for d in (2, 1, 3):
            send(G.at[q, y], G.at[q, y], s_gy[q][d], dev_y((y + d) % 4))

    def j_(q):
        h, a, e = CHUNKS[q]
        for d in range(1, 4):
            landed(G.at[q, (y + 4 - d) % 4], s_gy[q][d])
        out = lax.dot_general(
            G[q].reshape(16 * ROWS, 384), W[...], (((1,), (1,)), ((), ())), preferred_element_type=F32)
        IG[q] = out.astype(BF16).reshape(2, 2, 4, ROWS, 384)
        if e == 1:
            send(IG.at[q], RC.at[h, a], s_ic[h][a], other)

    def l_(k):
        h, a = k // 2, k % 2
        landed(RC.at[h, a], s_ic[h][a])
        both = IG[CHUNKS.index((h, a, 0))].astype(F32) + RC[h, a].astype(F32)
        for i in range(2):
            IX[h, a, i] = both[:, i].astype(BF16)
        for d in ((2,) if a == 0 else (1, 3)):
            v = (x + d) % 4
            send(IX.at[h, a, v // 2], RX.at[h, d - 1], s_ix[h][d], dev_x(v))

    def n_(h):
        total = IX[h, 0, x1].astype(F32)
        for d in range(1, 4):
            landed(RX.at[h, d - 1], s_ix[h][d])
            total = total + RX[h, d - 1].astype(F32)
        K[h] = total.astype(BF16)
        for d in range(1, 8):
            t = (zl + d) % 8
            send(K.at[h, t % 2, t // 2], RL.at[h, d - 1], s_out[h][d], dev_zl(t))

    def o_(h):
        total = K[h, z0, zq].astype(F32)
        for d in range(1, 8):
            landed(RL.at[h, d - 1], s_out[h][d])
            total = total + RL[h, d - 1].astype(F32)
        ig_ref[pl.ds(h * ROWS, ROWS), :] = total.astype(BF16)

    def w_(q):
        h, t, s = tok(q)
        rows = G[q].reshape(16 * ROWS, 384)
        wg_ref[...] += lax.dot_general(
            X[h, t, s].reshape(16 * ROWS, 384), rows, (((0,), (0,)), ((), ())), preferred_element_type=F32)
        BG[...] += jnp.sum(rows.astype(F32), axis=0, keepdims=True)

    def zs(h):
        for d in range(1, 8):
            send(x_hbm.at[pl.ds(h * ROWS, ROWS)], X.at[h, c, x0, z0, x1, zq], s_in[h][d], dev_zl((zl + d) % 8))

    zs(0)
    wg_ref[...] = jnp.zeros_like(wg_ref)
    BG[...] = jnp.zeros_like(BG)
    tasks = {"zs": zs, "zw": zw, "xa": xa, "xb": xb, "b": b, "d": d_, "e": e_, "f": f_, "g": g_, "h": h_,
             "j": j_, "l": l_, "n": n_, "o": o_, "w": w_}
    for task in ORDER[:-1]:
        tasks[task[:-1]](int(task[-1]))
    bg_ref[...] = BG[...].reshape(384)
    for d in sent:
        d.wait_send()
    tasks[ORDER[-1][:-1]](int(ORDER[-1][-1]))


def body(inputs, act_grad, w_in, bias_in):
    vm = lambda *s: pltpu.VMEM(s, BF16)
    nq, n = len(CHUNKS), 180
    return pl.pallas_call(
        kernel,
        out_shape=(
            jax.ShapeDtypeStruct((2 * ROWS, 384), BF16),
            jax.ShapeDtypeStruct((384, 384), F32),
            jax.ShapeDtypeStruct((384,), F32),
        ),
        in_specs=[pl.BlockSpec(memory_space=pl.ANY)] * 4,
        out_specs=[pl.BlockSpec(memory_space=pltpu.VMEM)] * 3,
        scratch_shapes=[
            vm(128, 384),
            vm(384, 384),
            pltpu.VMEM((384,), F32),
            vm(2, 2, 2, 2, 2, 4, ROWS, 384),
            vm(nq, 4, 4, ROWS, 384),
            vm(nq, 3, 4, ROWS, 384),
            vm(nq, 4, ROWS, 384),
            vm(nq, 3, ROWS, 384),
            vm(nq, ROWS, 384),
            vm(nq, 4, 4, ROWS, 384),
            vm(nq, 2, 2, 4, ROWS, 384),
            vm(2, 2, 2, 2, 4, ROWS, 384),
            vm(2, 2, 2, 2, 4, ROWS, 384),
            vm(2, 3, 2, 4, ROWS, 384),
            vm(2, 2, 4, ROWS, 384),
            vm(2, 7, ROWS, 384),
            pltpu.VMEM((1, 384), F32),
            pltpu.SemaphoreType.DMA((5,)),
            pltpu.SemaphoreType.DMA((n,)),
            pltpu.SemaphoreType.DMA((n,)),
        ],
        compiler_params=pltpu.CompilerParams(
            collective_id=0, has_side_effects=True, vmem_limit_bytes=56 * 1024 * 1024
        ),
    )(inputs, act_grad, w_in, bias_in)


def solution(mesh):
    return jax.shard_map(
        body,
        mesh=mesh,
        in_specs=(P("dp", "mp"), P("mp", "dp"), P("mp", "dp"), P("dp")),
        out_specs=(P("dp", "mp"), P("mp", "dp"), P("dp")),
        check_vma=False,
    )
```
